512 devices in a mesh: particle: 16 (over y, x), seq: 32 (over z, core).
Axes of the slice: x: 4, y: 4, z: 16, core: 2. Of those that a mesh axis runs over, the one named last changes fastest.
Arguments:
- latents: bfloat16 [32, 4096, 1536], P('particle', 'seq'), may hold values from -6 to 6
- mod_table: float32 [28, 3072], replicated, may hold values from -3 to 3
- step_index: int32 [1], replicated, may hold values from 0 to 27
- qkv_weight: bfloat16 [1536, 3072], P(('particle', 'seq')), may hold values from -0.15625 to 0.15625
- text_kv: bfloat16 [64, 154, 128], replicated, may hold values from -400 to 400
- ancestors: int32 [32], replicated, may hold values from 0 to 31, as said below
Outputs:
- attended: bfloat16 [32, 4096, 1024], P('particle', 'seq')
The draws below stay inside these ranges and needn't reach their ends.
Inputs may be any that keep to these rules, and one draw needn't show every extreme that they name: ancestors[d] lies in the same block of 8 consecutive particles as d; within each block the ancestors do not decrease, and the block's first and last particles are their own ancestors.
All inputs are finite; a program needn't handle non-finite values.
Results may differ from the reference program's by a relative error of at most 0.0059.
The reference program's roundings to bfloat16 on the way count: a program that leaves them out, or rounds other values in their place, can miss the bound.
Values may be sent and summed in bfloat16 or wider, within the bound.
A program may use at most 128 MiB of HBM per device.

```python
import jax
import jax.numpy as jnp
from jax import lax

D = 1536
HEADS = 16
HD = 64
IMG = 4096
TXT = 154
STEPS = 28
PER_PROMPT = 8
PARTICLES = 32
PROMPTS = 4


def draw_text_kv(key, part):
    key = jax.random.fold_in(key, 11)
    rows = PROMPTS * HEADS
    base = jnp.clip(jax.random.normal(key, (rows, TXT, 2 * HD), jnp.float32), -6.0, 6.0)
    keys = base[:, :, 0:HD]
    values = base[:, :, HD:2 * HD]
    return jnp.concatenate([keys, values], axis=2).astype(jnp.bfloat16)


def draw_ancestors(key, part):
    key = jax.random.fold_in(key, 23)
    key_hero, key_pick, key_rand = jax.random.split(key, 3)
    prompts = PARTICLES // PER_PROMPT
    hero = jax.random.randint(key_hero, (prompts, 1), 0, PER_PROMPT)
    pick = jax.random.randint(key_pick, (prompts, PER_PROMPT), 0, 2)
    spread = jax.random.randint(key_rand, (prompts, PER_PROMPT), 0, PER_PROMPT)
    chosen = jnp.where(pick == 1, hero, spread)
    chosen = chosen.at[:, 0].set(0)
    chosen = chosen.at[:, PER_PROMPT - 1].set(PER_PROMPT - 1)
    chosen = jnp.sort(chosen, axis=1)
    offsets = (jnp.arange(prompts, dtype=jnp.int32) * PER_PROMPT)[:, None]
    return (chosen + offsets).reshape(PARTICLES).astype(jnp.int32)


def levels(rng, shape, cuts, low, top_value):
    factor_of, own = 1.0, jax.random.fold_in(rng, 6)
    for position, shards_of in cuts:
        steps = jnp.exp(jax.random.uniform(jax.random.fold_in(own, position), (shards_of,), jnp.float32, low / len(cuts), top_value / len(cuts)))
        factor_of = factor_of * jnp.repeat(steps, shape[position] // shards_of).reshape([-1 if axis == position else 1 for axis in range(len(shape))])
    return factor_of


def noise(stream_key, extent, scale, most, pieces=(), kind=jnp.bfloat16):
    loudness = levels(stream_key, extent, pieces, -0.22, 0.18) if pieces else 1.0
    array = jax.random.normal(stream_key, extent, jnp.float32) * scale * loudness
    return jnp.minimum(jnp.maximum(array, -most), most).astype(kind)


def setup_inputs(seed: int = 0) -> dict:
    splits = jax.random.split(jax.random.key(seed), 7)
    latents = noise(splits[0], (PARTICLES, IMG, D), 1.0, 6.0, ((0, 16), (1, 32)))
    mod_table = noise(splits[1], (STEPS, 2 * D), 0.5, 3.0, (), jnp.float32)
    step_index = jax.random.randint(splits[2], (1,), 0, STEPS).astype(jnp.int32)
    qkv_weight = noise(splits[3], (D, 3 * HEADS * HD), D ** -0.5, 0.15625, ((0, 512),))
    text_kv = draw_text_kv(jax.random.fold_in(splits[6], 71), 0)
    ancestors = draw_ancestors(jax.random.fold_in(splits[6], 71), 0)
    return {"latents": latents, "mod_table": mod_table, "step_index": step_index, "qkv_weight": qkv_weight, "text_kv": text_kv, "ancestors": ancestors}


def modulate(rows, shift, scale):
    values = rows.astype(jnp.float32)
    mean = lax.optimization_barrier(jnp.mean(values, axis=-1, keepdims=True))
    centred = values - mean
    var = lax.optimization_barrier(jnp.mean(centred * centred, axis=-1, keepdims=True))
    normed = centred / jnp.sqrt(var + 1e-06)
    return (normed * (1.0 + scale) + shift).astype(jnp.bfloat16)

def attend_head(item_qkv, item_text):
    query = item_qkv[:, 0:HD]
    keys = jnp.concatenate([item_qkv[:, HD:2 * HD], item_text[:, 0:HD]], axis=0)
    values = jnp.concatenate([item_qkv[:, 2 * HD:3 * HD], item_text[:, HD:2 * HD]], axis=0)
    scores = jnp.dot(query, keys.T, preferred_element_type=jnp.float32) * HD ** (-0.5)
    expo = jnp.exp(scores - lax.optimization_barrier(jnp.max(scores, axis=-1, keepdims=True)))
    total = lax.optimization_barrier(jnp.sum(expo, axis=-1, keepdims=True))
    mixed = jnp.dot(expo.astype(jnp.bfloat16), values, preferred_element_type=jnp.float32)
    return (mixed / total).astype(jnp.bfloat16)

def reference(latents, mod_table, step_index, qkv_weight, text_kv, ancestors):
    select = (jnp.arange(STEPS, dtype=jnp.int32) == step_index[0]).astype(jnp.float32)
    modrow = lax.optimization_barrier(jnp.sum(mod_table * select[:, None], axis=0))
    shift = modrow[0:D]
    scale = modrow[D:2 * D]
    text_items = text_kv.reshape(PROMPTS, HEADS, TXT, 2 * HD)
    prompt_of = (jnp.arange(PARTICLES, dtype=jnp.int32) // PER_PROMPT).astype(jnp.int32)

    def one_particle(args):
        source, prompt = args
        rows = lax.dynamic_index_in_dim(latents, source, 0, keepdims=False)
        texts = lax.dynamic_index_in_dim(text_items, prompt, 0, keepdims=False)
        modded = modulate(rows, shift, scale)
        qkv = jnp.dot(modded, qkv_weight, preferred_element_type=jnp.float32).astype(jnp.bfloat16)
        qkv = qkv.reshape(IMG, HEADS, 3 * HD).transpose(1, 0, 2)
        heads_out = lax.map(lambda pair: attend_head(pair[0], pair[1]), (qkv, texts))
        return heads_out.transpose(1, 0, 2).reshape(IMG, HEADS * HD)
    return lax.map(one_particle, (ancestors.astype(jnp.int32), prompt_of))
```

```python
import functools

import jax
import jax.numpy as jnp
from jax import lax
from jax.experimental import pallas as pl
from jax.experimental.pallas import tpu as pltpu
from jax.sharding import PartitionSpec as P

HEADS = 16
HD = 64
PER_PROMPT = 8
MESH = pl.DeviceIdType.MESH
KEYS = 256
LOG2E = 1.4426950408889634


def low_lanes(shape):
    return lax.broadcasted_iota(jnp.int32, shape, len(shape) - 1) < HD


def swap_halves(value):
    return pltpu.roll(value, HD, len(value.shape) - 1)


def send(src, dst, send_sem, recv_sem, column, seq):
    return pltpu.make_async_remote_copy(
        src_ref=src, dst_ref=dst, send_sem=send_sem, recv_sem=recv_sem,
        device_id=(column, seq), device_id_type=MESH,
    )


def block_kernel(
    cols, ring, columns, seqs, txt,
    anc_ref, lat_ref, mod_ref, weight_ref, text_ref, out_ref,
    mod_all, wbuf, kv_out, q_out, kv_all, q_all, scores, o_out, o_all, chosen,
    x_send, x_recv, w_send, w_recv, kv_send, kv_recv, q_send, q_recv, o_send, o_recv, f_send, f_recv,
):
    part_dev, rows, width = lat_ref.shape
    particles = ring * part_dev
    half = rows // 2
    column, me = lax.axis_index("particle"), lax.axis_index("seq")
    first, x = column // ring * ring, column % ring
    left, right = first + (x + ring - 1) % ring, first + (x + 1) % ring
    wrows = weight_ref.shape[1]

    barrier = pltpu.get_barrier_semaphore()

    def greet_seq(k, _):
        pl.semaphore_signal(barrier, inc=1, device_id=(column, (me + k) % seqs), device_id_type=MESH)
        return 0

    def greet_column(k, _):
        pl.semaphore_signal(barrier, inc=1, device_id=((column + k) % columns, me), device_id_type=MESH)
        return 0

    lax.fori_loop(1, seqs, greet_seq, 0)
    lax.fori_loop(1, columns, greet_column, 0)
    pl.semaphore_wait(barrier, seqs + columns - 2)

    def weight_copy(k):
        other = (column + k) % columns
        return send(
            weight_ref.at[other % ring], wbuf.at[pl.ds(pl.multiple_of(column * wrows, wrows), wrows)],
            w_send.at[k], w_recv.at[column], other, me,
        )

    def weight_start(k, _):
        weight_copy(k).start()
        return 0

    lax.fori_loop(1, columns, weight_start, 0)
    own_weight = pltpu.make_async_copy(
        weight_ref.at[x], wbuf.at[pl.ds(pl.multiple_of(column * wrows, wrows), wrows)], w_send.at[0])
    own_weight.start()

    def slot(offset, part):
        return ((x + offset + ring) % ring) * part_dev + part

    def ring_copy(offset, part, leg, target):
        ref = mod_all.at[slot(offset, part)]
        return send(ref, ref, x_send.at[leg, part], x_recv.at[leg, part], target, me)

    shift, scale = mod_ref[0:1, 0:width], mod_ref[0:1, width:2 * width]
    for part in range(part_dev):
        values = lat_ref[part].astype(jnp.float32)
        mean = jnp.mean(values, axis=-1, keepdims=True)
        centred = values - mean
        var = jnp.mean(centred * centred, axis=-1, keepdims=True)
        normed = centred / jnp.sqrt(var + 1e-06)
        mod_all[slot(0, part)] = (normed * (1.0 + scale) + shift).astype(jnp.bfloat16)
        ring_copy(0, part, 0, right).start()
        ring_copy(0, part, 1, left).start()

    def item_seq(part, head):
        return head * particles + part

    def kv_copy(part, head):
        return send(
            kv_out.at[part, head], kv_all.at[pl.ds(pl.multiple_of(me * rows, rows), rows)],
            kv_send.at[item_seq(part, head)], kv_recv.at[me], column, item_seq(part, head),
        )

    def q_copy(part, head):
        return send(
            q_out.at[part, head], q_all.at[me],
            q_send.at[item_seq(part, head)], q_recv.at[me], column, item_seq(part, head),
        )

    def post(copy, own, part, head):
        target = item_seq(part, head)

        @pl.when(target != me)
        def _():
            copy(part, head).start()

        @pl.when(target == me)
        def _():
            own(part, head).start()

    def kv_own(part, head):
        return pltpu.make_async_copy(
            kv_out.at[part, head], kv_all.at[pl.ds(pl.multiple_of(me * rows, rows), rows)], kv_recv.at[me])

    def q_own(part, head):
        return pltpu.make_async_copy(q_out.at[part, head], q_all.at[me], q_recv.at[me])

    def project(offset):
        base = slot(offset, 0)
        states = mod_all[pl.ds(base, part_dev)].reshape(part_dev * rows, width)
        for group in range(cols // 2):
            lanes = slice((cols // 2) * 128 + group * 256, (cols // 2) * 128 + (group + 1) * 256)
            kv = jnp.dot(states, wbuf[:, lanes], preferred_element_type=jnp.float32)
            for part in range(part_dev):
                for side in range(2):
                    piece = kv[part * rows:(part + 1) * rows, side * 128:(side + 1) * 128]
                    kv_out[base + part, 2 * group + side] = piece.astype(jnp.bfloat16)
                    post(kv_copy, kv_own, base + part, 2 * group + side)
        query = jnp.dot(states, wbuf[:, 0:(cols // 2) * 128], preferred_element_type=jnp.float32)
        low = low_lanes((half, 128))
        for part in range(part_dev):
            for group in range(cols // 2):
                lanes = slice(group * 128, (group + 1) * 128)
                upper = query[part * rows:part * rows + half, lanes]
                lower = query[part * rows + half:(part + 1) * rows, lanes]
                q_out[base + part, 2 * group] = jnp.where(low, upper, swap_halves(lower)).astype(jnp.bfloat16)
                q_out[base + part, 2 * group + 1] = jnp.where(low, swap_halves(upper), lower).astype(jnp.bfloat16)

    own_weight.wait()

    def weight_wait(k, _):
        copy = send(
            weight_ref.at[0], wbuf.at[pl.ds(pl.multiple_of(((column + k) % columns) * wrows, wrows), wrows)],
            w_send.at[k], w_recv.at[(column + k) % columns], column, me)
        copy.wait_recv()
        return 0

    lax.fori_loop(1, columns, weight_wait, 0)
    project(0)
    for part in range(part_dev):
        ring_copy(-1, part, 0, right).wait_recv()
        ring_copy(1, part, 1, left).wait_recv()
    ring_copy(-1, 0, 2, right).start()
    ring_copy(1, 1, 2, left).start()
    project(-1)
    project(1)
    for part in range(part_dev):
        ring_copy(2, part, 2, right).wait_recv()
    project(2)
    for offset in (0, -1, 1, 2):
        for part in range(part_dev):
            for head in range(cols):
                post(q_copy, q_own, slot(offset, part), head)

    image = seqs * rows
    kv_all[image:image + KEYS] = text_ref[...]

    def kv_wait(k, _):
        src = (me + k) % seqs
        send(
            kv_out.at[0, 0], kv_all.at[pl.ds(pl.multiple_of(src * rows, rows), rows)],
            kv_send.at[0], kv_recv.at[src], column, me).wait_recv()
        return 0

    lax.fori_loop(0, seqs, kv_wait, 0)

    block = 2 * rows
    chunks = image // KEYS + 1
    factor = HD ** (-0.5) * LOG2E

    def o_copy(src, target):
        return send(o_out.at[src], o_all.at[me], o_send.at[src], o_recv.at[me], column, target)

    def attend(step, _):
        pair = (me // 2 + step) % (seqs // 2)
        queries = []
        low = low_lanes((half, 128))
        for side in range(2):
            src = 2 * pair + side
            send(q_out.at[0, 0], q_all.at[src], q_send.at[0], q_recv.at[src], column, me).wait_recv()
            packed = q_all[src].astype(jnp.float32)
            queries.append(jnp.where(low, packed, 0.0).astype(jnp.bfloat16))
            queries.append(jnp.where(low, swap_halves(packed), 0.0).astype(jnp.bfloat16))
        query = jnp.concatenate(queries, axis=0)
        top = jnp.full((block, 128), -jnp.inf, jnp.float32)
        for chunk in range(chunks):
            keys = kv_all[chunk * KEYS:(chunk + 1) * KEYS]
            part_scores = lax.dot_general(
                query, keys, (((1,), (1,)), ((), ())), preferred_element_type=jnp.float32)
            if chunk == chunks - 1:
                lane = lax.broadcasted_iota(jnp.int32, part_scores.shape, 1)
                part_scores = jnp.where(lane < txt, part_scores, -jnp.inf)
            scores[:, chunk * KEYS:(chunk + 1) * KEYS] = part_scores
            for piece in range(KEYS // 128):
                top = jnp.maximum(top, part_scores[:, piece * 128:(piece + 1) * 128])
        top = jnp.max(top, axis=1, keepdims=True)
        total = jnp.zeros((block, 128), jnp.float32)
        mixed = jnp.zeros((block, 128), jnp.float32)
        for chunk in range(chunks):
            expo = jnp.exp2((scores[:, chunk * KEYS:(chunk + 1) * KEYS] - top) * factor)
            for piece in range(KEYS // 128):
                total = total + expo[:, piece * 128:(piece + 1) * 128]
            mixed = mixed + jnp.dot(
                expo.astype(jnp.bfloat16), kv_all[chunk * KEYS:(chunk + 1) * KEYS],
                preferred_element_type=jnp.float32)
        result = mixed / jnp.sum(total, axis=1, keepdims=True)
        for side in range(2):
            target = 2 * pair + side
            upper = result[side * rows:side * rows + half]
            lower = result[side * rows + half:(side + 1) * rows]
            o_out[target] = jnp.where(low, swap_halves(upper), lower).astype(jnp.bfloat16)

            @pl.when(target != me)
            def _():
                o_copy(target, target).start()

            @pl.when(target == me)
            def _():
                pltpu.make_async_copy(o_out.at[target], o_all.at[me], o_recv.at[me]).start()
        return 0

    lax.fori_loop(0, seqs // 2, attend, 0)

    def o_wait(k, _):
        src = (me + k) % seqs
        send(o_out.at[0], o_all.at[src], o_send.at[0], o_recv.at[src], column, me).wait_recv()
        return 0

    lax.fori_loop(0, seqs, o_wait, 0)
    low = low_lanes((half, 128))

    def final_copy(k):
        lanes = pl.ds(pl.multiple_of(x * (cols * HD), 128), cols * HD)
        return send(
            chosen.at[k], out_ref.at[:, :, lanes], f_send.at[k], f_recv.at[(ring - k) % ring],
            first + (x + k) % ring, me)

    for k in (2, 1, 3, 0):
        goal = (x + k) % ring
        for part in range(part_dev):
            source = anc_ref[(first + goal) * part_dev + part] % particles
            for group in range(cols // 2):
                even = o_all[2 * group * particles + source].astype(jnp.float32)
                odd = o_all[(2 * group + 1) * particles + source].astype(jnp.float32)
                lanes = slice(group * 128, (group + 1) * 128)
                chosen[k, part, 0:half, lanes] = jnp.where(low, even, swap_halves(odd)).astype(jnp.bfloat16)
                chosen[k, part, half:rows, lanes] = jnp.where(low, swap_halves(even), odd).astype(jnp.bfloat16)
        if k:
            final_copy(k).start()
    own_final = pltpu.make_async_copy(
        chosen.at[0], out_ref.at[:, :, pl.ds(pl.multiple_of(x * (cols * HD), 128), cols * HD)], f_send.at[0])
    own_final.start()
    own_final.wait()

    for part in range(part_dev):
        ring_copy(0, part, 0, right).wait_send()
        ring_copy(0, part, 1, left).wait_send()
    ring_copy(-1, 0, 2, right).wait_send()
    ring_copy(1, 1, 2, left).wait_send()

    def weight_sent(k, _):
        weight_copy(k).wait_send()
        return 0

    lax.fori_loop(1, columns, weight_sent, 0)

    def item_sent(k, _):
        target = (me + k) % seqs
        part, head = target % particles, target // particles
        kv_copy(part, head).wait_send()
        q_copy(part, head).wait_send()
        o_copy(target, target).wait_send()
        return 0

    lax.fori_loop(1, seqs, item_sent, 0)
    for k in range(1, ring):
        final_copy(k).wait_send()
        lanes = pl.ds(pl.multiple_of((x + k) % ring * (cols * HD), 128), cols * HD)
        send(
            chosen.at[k], out_ref.at[:, :, lanes], f_send.at[k], f_recv.at[k],
            column, me).wait_recv()


def local(columns, seqs, latents, mod_table, step_index, qkv_weight, text_kv, ancestors):
    part_dev, rows, width = latents.shape
    ring = PER_PROMPT // part_dev
    cols = HEADS // ring
    txt = text_kv.shape[1]
    column, me = lax.axis_index("particle"), lax.axis_index("seq")
    modrow = lax.dynamic_slice_in_dim(mod_table, step_index[0], 1, 0)
    wrows = qkv_weight.shape[0]
    by_head = qkv_weight.reshape(wrows, ring, cols, 3 * HD)
    arranged = jnp.concatenate([
        by_head[..., 0:HD].reshape(wrows, ring, cols * HD),
        by_head[..., HD:3 * HD].reshape(wrows, ring, 2 * cols * HD),
    ], axis=2).reshape(wrows, ring * 3 * cols * HD)
    weight = lax.all_gather(arranged, "seq", axis=0, tiled=True)
    weight = weight.reshape(seqs * wrows, ring, 3 * cols * HD).transpose(1, 0, 2)
    text_row = column // ring * HEADS + column % ring * cols + me // PER_PROMPT
    text = lax.dynamic_index_in_dim(text_kv, text_row, 0, keepdims=False)
    text = jnp.pad(text, ((0, KEYS - txt), (0, 0)))
    items = PER_PROMPT * cols
    chunks = seqs * rows // KEYS + 1
    bf16, f32 = jnp.bfloat16, jnp.float32
    vmem, dma = pltpu.VMEM, pltpu.SemaphoreType.DMA
    return pl.pallas_call(
        functools.partial(block_kernel, cols, ring, columns, seqs, txt),
        out_shape=jax.ShapeDtypeStruct((part_dev, rows, HEADS * HD), bf16),
        in_specs=[pl.BlockSpec(memory_space=pltpu.SMEM)] + [pl.BlockSpec(memory_space=pltpu.VMEM)] * 4,
        out_specs=pl.BlockSpec(memory_space=pltpu.VMEM),
        scratch_shapes=[
            vmem((PER_PROMPT, rows, width), bf16),
            vmem((columns * seqs * wrows, 3 * cols * HD), bf16),
            vmem((PER_PROMPT, cols, rows, 128), bf16),
            vmem((PER_PROMPT, cols, rows // 2, 128), bf16),
            vmem((seqs * rows + KEYS, 128), bf16),
            vmem((seqs, rows // 2, 128), bf16),
            vmem((2 * rows, chunks * KEYS), f32),
            vmem((seqs, rows // 2, 128), bf16),
            vmem((seqs, rows // 2, 128), bf16),
            vmem((ring, part_dev, rows, cols * HD), bf16),
            dma((3, part_dev)), dma((3, part_dev)),
            dma((columns,)), dma((columns,)),
            dma((items,)), dma((items,)), dma((items,)), dma((items,)), dma((items,)), dma((items,)),
            dma((ring,)), dma((ring,)),
        ],
        compiler_params=pltpu.CompilerParams(
            collective_id=0, has_side_effects=True, vmem_limit_bytes=48 * 2**20),
        cost_estimate=pl.CostEstimate(flops=7 * 10**9, bytes_accessed=4 * 10**6, transcendentals=18 * 10**6),
        name="steered_block",
    )(ancestors, latents, modrow, weight, text)


def solution(mesh):
    in_specs = (P("particle", "seq", None), P(), P(), P(("particle", "seq"), None), P(), P())
    out_specs = P("particle", "seq", None)
    body = functools.partial(local, mesh.shape["particle"], mesh.shape["seq"])
    return jax.shard_map(body, mesh=mesh, in_specs=in_specs, out_specs=out_specs, check_vma=False)
```

```python
import functools

import jax
import jax.numpy as jnp
from jax import lax
from jax.experimental import pallas as pl
from jax.experimental.pallas import tpu as pltpu
from jax.sharding import PartitionSpec as P

HEADS = 16
HD = 64
PER_PROMPT = 8
MESH = pl.DeviceIdType.MESH
KEYS = 256
FORWARD_AT = 4
TEXT_PAD = 160
SLICES = 4
ROW_PAD = 8
LOG2E = 1.4426950408889634


def low_lanes(shape):
    return lax.broadcasted_iota(jnp.int32, shape, len(shape) - 1) < HD


def swap_halves(value):
    return pltpu.roll(value, HD, len(value.shape) - 1)


def send(src, dst, send_sem, recv_sem, column, seq):
    return pltpu.make_async_remote_copy(
        src_ref=src, dst_ref=dst, send_sem=send_sem, recv_sem=recv_sem,
        device_id=(column, seq), device_id_type=MESH,
    )


def pack_weight(weight_ref, wsend, ring, cols):
    shard = weight_ref[...].astype(jnp.float32)
    count = shard.shape[0]
    for r in range(ring):
        for group in range(3 * cols // 2):
            if group < cols // 2:
                start = (r * cols + 2 * group) * 3 * HD
                piece = jnp.concatenate([shard[:, start:start + HD], shard[:, start + 3 * HD:start + 4 * HD]], axis=1)
            else:
                start = (r * cols + group - cols // 2) * 3 * HD + HD
                piece = shard[:, start:start + 2 * HD]
            for i in range(count):
                wsend[r, i, group:group + 1, :] = piece[i:i + 1]


def block_kernel(
    cols, ring, columns, seqs, txt,
    anc_ref, step_ref, lat_ref, mod_ref, weight_ref, text_hbm, out_ref,
    mod_all, order, wsend, wplane, wbuf, kv_out, q_out, kv_all, values_t, q_all, text_buf,
    scores, probs, o_out, o_all, chosen,
    x_send, x_recv, p_send, p_recv, w_send, w_recv, t_sem,
    kv_send, kv_recv, q_send, q_recv, o_send, o_recv, f_send, f_recv,
):
    part_dev, rows, width = lat_ref.shape
    particles = ring * part_dev
    half = rows // 2
    column, me = lax.axis_index("particle"), lax.axis_index("seq")
    first, x = column // ring * ring, column % ring
    left, right = first + (x + ring - 1) % ring, first + (x + 1) % ring
    wrows = weight_ref.shape[0]
    image = seqs * rows

    barrier = pltpu.get_barrier_semaphore()

    def greet_seq(k, _):
        pl.semaphore_signal(barrier, inc=1, device_id=(column, (me + k) % seqs), device_id_type=MESH)
        return 0

    def greet_column(k, _):
        pl.semaphore_signal(barrier, inc=1, device_id=((column + k) % columns, me), device_id_type=MESH)
        return 0

    lax.fori_loop(1, seqs, greet_seq, 0)
    lax.fori_loop(1, columns, greet_column, 0)

    text_row = column // ring * HEADS + x * cols + me // particles
    text_copy = pltpu.make_async_copy(text_hbm.at[text_row], text_buf, t_sem)
    text_copy.start()
    pack_weight(weight_ref, wsend, ring, cols)
    span = seqs * wrows
    local_row = lax.broadcasted_iota(jnp.int32, (span, 1), 0)
    owner = lax.shift_right_logical(local_row * 43691, 17)
    place = owner * (wrows * columns) + (local_row - owner * wrows) * columns
    lane = lax.broadcasted_iota(jnp.int32, (span, width), 1)
    for c in range(columns):
        order[c * span:(c + 1) * span] = jnp.where(lane == place + c, 1.0, 0.0).astype(jnp.bfloat16)
    pl.semaphore_wait(barrier, seqs + columns - 2)

    def plane_copy(k):
        other = (column + k) % columns
        return send(wsend.at[other % ring], wplane.at[column], p_send.at[k], p_recv.at[column], other, me)

    def plane_start(k, _):
        plane_copy(k).start()
        return 0

    lax.fori_loop(1, columns, plane_start, 0)
    plane_own = pltpu.make_async_copy(wsend.at[x], wplane.at[column], p_recv.at[column])
    plane_own.start()

    def slot(offset, part):
        return ((x + offset + ring) % ring) * part_dev + part

    def ring_copy(offset, part, leg, target):
        ref = mod_all.at[slot(offset, part)]
        return send(ref, ref, x_send.at[leg, part], x_recv.at[leg, part], target, me)

    mod_row = mod_ref[pl.ds(step_ref[0], 1), :]
    shift, scale = mod_row[:, 0:width], mod_row[:, width:2 * width]
    for part in range(part_dev):
        values = lat_ref[part].astype(jnp.float32)
        mean = jnp.mean(values, axis=-1, keepdims=True)
        centred = values - mean
        var = jnp.mean(centred * centred, axis=-1, keepdims=True)
        normed = centred / jnp.sqrt(var + 1e-06)
        modded = (normed * (1.0 + scale) + shift).astype(jnp.bfloat16)
        mod_all[slot(0, part)] = jnp.dot(modded, order[...], preferred_element_type=jnp.float32).astype(jnp.bfloat16)
    for part in range(part_dev):
        ring_copy(0, part, 0, right).start()
        ring_copy(0, part_dev - 1 - part, 1, left).start()

    def item_seq(part, head):
        return head * particles + part

    def kv_copy(part, head):
        return send(
            kv_out.at[part, head], kv_all.at[pl.ds(pl.multiple_of(me * rows, rows), rows)],
            kv_send.at[item_seq(part, head)], kv_recv.at[me], column, item_seq(part, head),
        )

    def q_copy(part, head):
        return send(
            q_out.at[part, head], q_all.at[me],
            q_send.at[item_seq(part, head)], q_recv.at[me], column, item_seq(part, head),
        )

    def post(copy, own, part, head):
        target = item_seq(part, head)

        @pl.when(target != me)
        def _():
            copy(part, head).start()

        @pl.when(target == me)
        def _():
            own(part, head).start()

    def kv_own(part, head):
        return pltpu.make_async_copy(
            kv_out.at[part, head], kv_all.at[pl.ds(pl.multiple_of(me * rows, rows), rows)], kv_recv.at[me])

    def q_own(part, head):
        return pltpu.make_async_copy(q_out.at[part, head], q_all.at[me], q_recv.at[me])

    def project(offset):
        base = slot(offset, 0)
        states = mod_all[pl.ds(base, part_dev)].reshape(part_dev * rows, width)
        for group in range(cols // 2):
            lanes = slice((cols // 2) * 128 + group * 256, (cols // 2) * 128 + (group + 1) * 256)
            kv = jnp.dot(states, wbuf[:, lanes], preferred_element_type=jnp.float32)
            for part in range(part_dev):
                for side in range(2):
                    piece = kv[part * rows:(part + 1) * rows, side * 128:(side + 1) * 128]
                    kv_out[base + part, 2 * group + side] = piece.astype(jnp.bfloat16)
                    post(kv_copy, kv_own, base + part, 2 * group + side)
        query = jnp.dot(states, wbuf[:, 0:(cols // 2) * 128], preferred_element_type=jnp.float32)
        low = low_lanes((half, 128))
        for part in range(part_dev):
            for group in range(cols // 2):
                lanes = slice(group * 128, (group + 1) * 128)
                upper = query[part * rows:part * rows + half, lanes]
                lower = query[part * rows + half:(part + 1) * rows, lanes]
                q_out[base + part, 2 * group] = jnp.where(low, upper, swap_halves(lower)).astype(jnp.bfloat16)
                q_out[base + part, 2 * group + 1] = jnp.where(low, swap_halves(upper), lower).astype(jnp.bfloat16)

    def plane_wait(k, _):
        src = (column + k) % columns
        send(wsend.at[0], wplane.at[src], p_send.at[k], p_recv.at[src], column, me).wait_recv()
        return 0

    lax.fori_loop(0, columns, plane_wait, 0)
    block_rows = wrows * columns

    def weight_rows(index):
        return wbuf.at[pl.ds(pl.multiple_of(index * block_rows, block_rows), block_rows)]

    base_row = pl.multiple_of(me * block_rows, block_rows)
    for group in range(3 * cols // 2):
        for i in range(wrows):
            wbuf[pl.ds(base_row + i * columns, columns), group * 128:(group + 1) * 128] = (
                wplane[:, i, group, :].astype(jnp.bfloat16))
    chips = seqs // 2
    sibling = me + 1 - 2 * (me % 2)

    def around(hops):
        return (me + 2 * hops + seqs) % seqs

    def weight_copy(index, leg, hop, target):
        return send(weight_rows(index), weight_rows(index), w_send.at[leg, hop], w_recv.at[index], column, target)

    def weight_wait(index):
        weight_copy(index, 0, 0, me).wait_recv()

    reach = (chips // 2, chips - 1 - chips // 2)
    started = []

    def weight_start(*args):
        copy = weight_copy(*args)
        copy.start()
        started.append(copy)

    weight_start(me, 0, 0, around(1))
    weight_start(me, 1, 0, around(-1))
    weight_start(me, 2, 0, sibling)
    for hop in range(1, reach[0] + 1):
        index = around(-hop)
        weight_wait(index)
        if hop < reach[0]:
            weight_start(index, 0, hop, around(1))
        weight_start(index, 2, hop, sibling)
        if hop <= reach[1]:
            index = around(hop)
            weight_wait(index)
            if hop < reach[1]:
                weight_start(index, 1, hop, around(-1))
            weight_start(index, 3, hop, sibling)
        if hop == FORWARD_AT:
            ring_copy(-1, 0, 0, right).wait_recv()
            ring_copy(-1, 0, 2, right).start()
            ring_copy(1, 1, 1, left).wait_recv()
            ring_copy(1, 1, 2, left).start()

    def sibling_wait(k, _):
        weight_wait((sibling + 2 * k) % seqs)
        return 0

    lax.fori_loop(0, chips, sibling_wait, 0)
    project(0)
    ring_copy(-1, 1, 0, right).wait_recv()
    ring_copy(1, 0, 1, left).wait_recv()
    project(-1)
    project(1)
    for part in range(part_dev):
        ring_copy(2, part, 2, right).wait_recv()
    project(2)
    for offset in (0, -1, 1, 2):
        for part in range(part_dev):
            for head in range(cols):
                post(q_copy, q_own, slot(offset, part), head)

    text_copy.wait()
    kv_all[image:image + TEXT_PAD] = jnp.zeros((TEXT_PAD, 128), jnp.bfloat16)
    kv_all[image:image + txt] = text_buf[...]

    def kv_wait(k, _):
        src = (me + k) % seqs
        send(
            kv_out.at[0, 0], kv_all.at[pl.ds(pl.multiple_of(src * rows, rows), rows)],
            kv_send.at[0], kv_recv.at[src], column, me).wait_recv()
        return 0

    lax.fori_loop(0, seqs, kv_wait, 0)

    joint = image + TEXT_PAD
    bounds = [(low, min(KEYS, joint - low)) for low in range(0, joint, KEYS)]
    for low, count in bounds:
        turned = kv_all[low:low + count].astype(jnp.float32).T
        values_t[:, low:low + count] = turned[HD:2 * HD].astype(jnp.bfloat16)

    block = SLICES * rows
    factor = HD ** (-0.5) * LOG2E

    def o_copy(src, target):
        return send(o_out.at[src], o_all.at[me], o_send.at[src], o_recv.at[me], column, target)

    def fold(value, op):
        result = value[0:8]
        for row in range(8, value.shape[0], 8):
            result = op(result, value[row:row + 8])
        return result

    def attend(step, _):
        base = (me // SLICES + step) % (seqs // SLICES) * SLICES
        queries = []
        lower_lanes = low_lanes((half, 128))
        for side in range(SLICES):
            src = base + side
            send(q_out.at[0, 0], q_all.at[src], q_send.at[0], q_recv.at[src], column, me).wait_recv()
            packed = q_all[src].astype(jnp.float32)
            queries.append(jnp.where(lower_lanes, packed, 0.0).astype(jnp.bfloat16))
            queries.append(jnp.where(lower_lanes, swap_halves(packed), 0.0).astype(jnp.bfloat16))
        query = jnp.concatenate(queries, axis=0)
        top = jnp.full((8, block), -jnp.inf, jnp.float32)
        for low, count in bounds:
            part_scores = lax.dot_general(
                kv_all[low:low + count], query, (((1,), (1,)), ((), ())), preferred_element_type=jnp.float32)
            if low + count > image + txt:
                key = lax.broadcasted_iota(jnp.int32, part_scores.shape, 0) + low
                part_scores = jnp.where(key < image + txt, part_scores, -jnp.inf)
            scores[low:low + count] = part_scores
            top = jnp.maximum(top, fold(part_scores, jnp.maximum))
        top = jnp.max(top, axis=0, keepdims=True)
        total = jnp.zeros((8, block), jnp.float32)
        for low, count in bounds:
            expo = jnp.exp2((scores[low:low + count] - top) * factor)
            total = total + fold(expo, jnp.add)
            probs[low:low + count] = expo.astype(jnp.bfloat16)
        mixed = jnp.dot(values_t[...], probs[...], preferred_element_type=jnp.float32)
        result = (mixed / jnp.sum(total, axis=0, keepdims=True)).T
        for side in range(SLICES):
            target = base + side
            upper = result[side * rows:side * rows + half]
            lower = result[side * rows + half:(side + 1) * rows]
            o_out[target] = jnp.concatenate([upper, lower], axis=1).astype(jnp.bfloat16)

            @pl.when(target != me)
            def _():
                o_copy(target, target).start()

            @pl.when(target == me)
            def _():
                pltpu.make_async_copy(o_out.at[target], o_all.at[me], o_recv.at[me]).start()
        return 0

    lax.fori_loop(0, seqs // SLICES, attend, 0)

    def o_wait(k, _):
        src = (me + k) % seqs
        send(o_out.at[0], o_all.at[src], o_send.at[0], o_recv.at[src], column, me).wait_recv()
        return 0

    lax.fori_loop(0, seqs, o_wait, 0)
    low = low_lanes((half, 128))

    def final_copy(k):
        lanes = pl.ds(pl.multiple_of(x * (cols * HD), 128), cols * HD)
        return send(
            chosen.at[k], out_ref.at[:, :, lanes], f_send.at[k], f_recv.at[(ring - k) % ring],
            first + (x + k) % ring, me)

    for k in (2, 1, 3, 0):
        goal = (x + k) % ring
        for part in range(part_dev):
            source = anc_ref[(first + goal) * part_dev + part] % particles
            for group in range(cols // 2):
                even = o_all[2 * group * particles + source].astype(jnp.float32)
                odd = o_all[(2 * group + 1) * particles + source].astype(jnp.float32)
                lanes = slice(group * 128, (group + 1) * 128)
                chosen[k, part, 0:half, lanes] = jnp.where(low, even, swap_halves(odd)).astype(jnp.bfloat16)
                chosen[k, part, half:rows, lanes] = jnp.where(low, swap_halves(even), odd).astype(jnp.bfloat16)
        if k:
            final_copy(k).start()
    own_final = pltpu.make_async_copy(
        chosen.at[0], out_ref.at[:, :, pl.ds(pl.multiple_of(x * (cols * HD), 128), cols * HD)], f_send.at[0])
    own_final.start()
    own_final.wait()

    for part in range(part_dev):
        ring_copy(0, part, 0, right).wait_send()
        ring_copy(0, part, 1, left).wait_send()
    ring_copy(-1, 0, 2, right).wait_send()
    ring_copy(1, 1, 2, left).wait_send()

    def plane_sent(k, _):
        plane_copy(k).wait_send()
        return 0

    lax.fori_loop(1, columns, plane_sent, 0)
    for copy in started:
        copy.wait_send()

    def item_sent(k, _):
        target = (me + k) % seqs
        part, head = target % particles, target // particles
        kv_copy(part, head).wait_send()
        q_copy(part, head).wait_send()
        o_copy(target, target).wait_send()
        return 0

    lax.fori_loop(1, seqs, item_sent, 0)
    for k in range(1, ring):
        final_copy(k).wait_send()
        lanes = pl.ds(pl.multiple_of((x + k) % ring * (cols * HD), 128), cols * HD)
        send(
            chosen.at[k], out_ref.at[:, :, lanes], f_send.at[k], f_recv.at[k],
            column, me).wait_recv()


def local(columns, seqs, latents, mod_table, step_index, qkv_weight, text_kv, ancestors):
    part_dev, rows, width = latents.shape
    ring = PER_PROMPT // part_dev
    cols = HEADS // ring
    txt = text_kv.shape[1]
    wrows = qkv_weight.shape[0]
    items = PER_PROMPT * cols
    joint = seqs * rows + TEXT_PAD
    bf16, f32 = jnp.bfloat16, jnp.float32
    vmem, dma = pltpu.VMEM, pltpu.SemaphoreType.DMA
    smem_spec, vmem_spec = pl.BlockSpec(memory_space=pltpu.SMEM), pl.BlockSpec(memory_space=pltpu.VMEM)
    return pl.pallas_call(
        functools.partial(block_kernel, cols, ring, columns, seqs, txt),
        out_shape=jax.ShapeDtypeStruct((part_dev, rows, HEADS * HD), bf16),
        in_specs=[smem_spec, smem_spec, vmem_spec, vmem_spec, vmem_spec, pl.BlockSpec(memory_space=pl.ANY)],
        out_specs=vmem_spec,
        scratch_shapes=[
            vmem((PER_PROMPT, rows, width), bf16),
            vmem((width, width), bf16),
            vmem((ring, wrows, ROW_PAD, 128), f32),
            vmem((columns, wrows, ROW_PAD, 128), f32),
            vmem((width, 3 * cols * HD), bf16),
            vmem((PER_PROMPT, cols, rows, 128), bf16),
            vmem((PER_PROMPT, cols, rows // 2, 128), bf16),
            vmem((joint, 128), bf16),
            vmem((HD, joint), bf16),
            vmem((seqs, rows // 2, 128), bf16),
            vmem((txt, 128), bf16),
            vmem((joint, SLICES * rows), f32),
            vmem((joint, SLICES * rows), bf16),
            vmem((seqs, rows // 2, 128), bf16),
            vmem((seqs, rows // 2, 128), bf16),
            vmem((ring, part_dev, rows, cols * HD), bf16),
            dma((3, part_dev)), dma((3, part_dev)),
            dma((columns,)), dma((columns,)),
            dma((4, seqs // 4 + 1)), dma((seqs,)), dma,
            dma((items,)), dma((items,)), dma((items,)), dma((items,)), dma((items,)), dma((items,)),
            dma((ring,)), dma((ring,)),
        ],
        compiler_params=pltpu.CompilerParams(
            collective_id=0, has_side_effects=True, vmem_limit_bytes=52 * 2**20),
        cost_estimate=pl.CostEstimate(flops=7 * 10**9, bytes_accessed=4 * 10**6, transcendentals=18 * 10**6),
        name="steered_block",
    )(ancestors, step_index, latents, mod_table, qkv_weight, text_kv)


def solution(mesh):
    in_specs = (P("particle", "seq", None), P(), P(), P(("particle", "seq"), None), P(), P())
    out_specs = P("particle", "seq", None)
    body = functools.partial(local, mesh.shape["particle"], mesh.shape["seq"])
    return jax.shard_map(body, mesh=mesh, in_specs=in_specs, out_specs=out_specs, check_vma=False)
```

```python
import functools

import jax
import jax.numpy as jnp
from jax import lax
from jax.experimental import pallas as pl
from jax.experimental.pallas import tpu as pltpu
from jax.sharding import PartitionSpec as P

HEADS = 16
HD = 64
PER_PROMPT = 8
MESH = pl.DeviceIdType.MESH
KEYS = 256
TEXT_PAD = 160
SLICES = 4
PIECES = 3
ROW_PAD = 8
LOG2E = 1.4426950408889634


def low_lanes(shape):
    return lax.broadcasted_iota(jnp.int32, shape, len(shape) - 1) < HD


def swap_halves(value):
    return pltpu.roll(value, HD, len(value.shape) - 1)


def send(src, dst, send_sem, recv_sem, column, seq):
    return pltpu.make_async_remote_copy(
        src_ref=src, dst_ref=dst, send_sem=send_sem, recv_sem=recv_sem,
        device_id=(column, seq), device_id_type=MESH,
    )


def pack_weight(weight_ref, wsend, ring, cols):
    shard = weight_ref[...].astype(jnp.float32)
    count = shard.shape[0]
    for r in range(ring):
        for group in range(3 * cols // 2):
            if group < cols // 2:
                start = (r * cols + 2 * group) * 3 * HD
                piece = jnp.concatenate([shard[:, start:start + HD], shard[:, start + 3 * HD:start + 4 * HD]], axis=1)
            else:
                start = (r * cols + group - cols // 2) * 3 * HD + HD
                piece = shard[:, start:start + 2 * HD]
            for i in range(count):
                wsend[r, i, group:group + 1, :] = piece[i:i + 1]


def block_kernel(
    cols, ring, columns, seqs, txt,
    step_ref, anc_any, lat_any, mod_any, weight_ref, text_hbm, out_ref,
    anc_ref, lat_ref, mod_ref, in_sem, mod_all, order, wsend, wplane, wbuf, kv_out, q_out, kv_all, values_t, q_all, text_buf,
    scores, probs, o_out, o_all, chosen,
    x_send, x_recv, p_send, p_recv, z_send, z_recv, y_send, y_recv, b_send, b_recv, t_sem,
    kv_send, kv_recv, q_send, q_recv, o_send, o_recv, f_send, f_recv,
):
    part_dev, rows, width = lat_ref.shape
    particles = ring * part_dev
    half = rows // 2
    column, me = lax.axis_index("particle"), lax.axis_index("seq")
    first, x = column // ring * ring, column % ring
    left, right = first + (x + ring - 1) % ring, first + (x + 1) % ring
    wrows = weight_ref.shape[0]
    image = seqs * rows

    inputs = [
        pltpu.make_async_copy(src, dst, in_sem.at[i])
        for i, (src, dst) in enumerate(((lat_any, lat_ref), (mod_any, mod_ref), (anc_any, anc_ref)))
    ]
    for copy in inputs:
        copy.start()

    barrier = pltpu.get_barrier_semaphore()

    def greet_seq(k, _):
        pl.semaphore_signal(barrier, inc=1, device_id=(column, (me + k) % seqs), device_id_type=MESH)
        return 0

    def greet_column(k, _):
        pl.semaphore_signal(barrier, inc=1, device_id=((column + k) % columns, me), device_id_type=MESH)
        return 0

    lax.fori_loop(1, seqs, greet_seq, 0)
    lax.fori_loop(1, columns, greet_column, 0)

    text_block = pl.ds(pl.multiple_of(column // ring * HEADS, HEADS), HEADS)
    text_copy = pltpu.make_async_copy(text_hbm.at[:, text_block, :], text_buf, t_sem)
    text_copy.start()
    pack_weight(weight_ref, wsend, ring, cols)
    span = seqs * wrows
    chips, planes = seqs // 2, columns // ring
    per = chips // planes
    y, z, core = column // ring, me // 2, me % 2

    def arrival(index):
        at = index // 2
        return index % 2 * chips + at % planes * per + at // planes

    local_row = lax.broadcasted_iota(jnp.int32, (span, 1), 0)
    owner = lax.shift_right_logical(local_row * 43691, 17)
    place = arrival(owner) * (wrows * columns) + (local_row - owner * wrows) * columns
    lane = lax.broadcasted_iota(jnp.int32, (span, width), 1)
    for c in range(columns):
        order[c * span:(c + 1) * span] = jnp.where(lane == place + c, 1.0, 0.0).astype(jnp.bfloat16)
    pl.semaphore_wait(barrier, seqs + columns - 2)

    def plane_copy(k):
        goal = (x + k) % ring
        return send(
            wsend.at[goal], wplane.at[column], p_send.at[k], p_recv.at[column], z % planes * ring + goal, me)

    for k in range(1, ring):
        plane_copy(k).start()

    @pl.when(z % planes != y)
    def _():
        plane_copy(0).start()

    @pl.when(z % planes == y)
    def _():
        pltpu.make_async_copy(wsend.at[x], wplane.at[column], p_recv.at[column]).start()

    def slot(offset, part):
        return ((x + offset + ring) % ring) * part_dev + part

    def ring_copy(offset, part, leg, target):
        ref = mod_all.at[slot(offset, part)]
        return send(ref, ref, x_send.at[leg, part], x_recv.at[leg, part], target, me)

    for copy in inputs:
        copy.wait()
    mod_row = mod_ref[pl.ds(step_ref[0], 1), :]
    shift, scale = mod_row[:, 0:width], mod_row[:, width:2 * width]
    for part in range(part_dev):
        values = lat_ref[part].astype(jnp.float32)
        mean = jnp.mean(values, axis=-1, keepdims=True)
        centred = values - mean
        var = jnp.mean(centred * centred, axis=-1, keepdims=True)
        normed = centred / jnp.sqrt(var + 1e-06)
        modded = (normed * (1.0 + scale) + shift).astype(jnp.bfloat16)
        mod_all[slot(0, part)] = jnp.dot(modded, order[...], preferred_element_type=jnp.float32).astype(jnp.bfloat16)
    for part in range(part_dev):
        ring_copy(0, part, 0, right).start()
        ring_copy(0, part_dev - 1 - part, 1, left).start()

    def item_seq(part, head):
        return head * particles + part

    def kv_copy(part, head):
        return send(
            kv_out.at[part, head], kv_all.at[pl.ds(pl.multiple_of(me * rows, rows), rows)],
            kv_send.at[item_seq(part, head)], kv_recv.at[me], column, item_seq(part, head),
        )

    def q_copy(part, head):
        return send(
            q_out.at[part, head], q_all.at[me],
            q_send.at[item_seq(part, head)], q_recv.at[me], column, item_seq(part, head),
        )

    def post(copy, own, part, head):
        target = item_seq(part, head)

        @pl.when(target != me)
        def _():
            copy(part, head).start()

        @pl.when(target == me)
        def _():
            own(part, head).start()

    def kv_own(part, head):
        return pltpu.make_async_copy(
            kv_out.at[part, head], kv_all.at[pl.ds(pl.multiple_of(me * rows, rows), rows)], kv_recv.at[me])

    def q_own(part, head):
        return pltpu.make_async_copy(q_out.at[part, head], q_all.at[me], q_recv.at[me])

    def project_kv(offset, group):
        base = slot(offset, 0)
        kv = jnp.dot(states_of(offset), wbuf[group], preferred_element_type=jnp.float32)
        for part in range(part_dev):
            for side in range(2):
                piece = kv[part * rows:(part + 1) * rows, side * 128:(side + 1) * 128]
                kv_out[base + part, 2 * group + side] = piece.astype(jnp.bfloat16)
                post(kv_copy, kv_own, base + part, 2 * group + side)

    def project_q(offset):
        base = slot(offset, 0)
        query = jnp.dot(states_of(offset), wbuf[PIECES - 1], preferred_element_type=jnp.float32)
        low = low_lanes((half, 128))
        for part in range(part_dev):
            for group in range(cols // 2):
                lanes = slice(group * 128, (group + 1) * 128)
                upper = query[part * rows:part * rows + half, lanes]
                lower = query[part * rows + half:(part + 1) * rows, lanes]
                q_out[base + part, 2 * group] = jnp.where(low, upper, swap_halves(lower)).astype(jnp.bfloat16)
                q_out[base + part, 2 * group + 1] = jnp.where(low, swap_halves(upper), lower).astype(jnp.bfloat16)

    def weight_place(group):
        if group < cols // 2:
            return PIECES - 1, slice(group * 128, (group + 1) * 128)
        head = group - cols // 2
        return head // 2, slice(head % 2 * 128, (head % 2 + 1) * 128)

    block_rows = wrows * columns

    def weight_ref_of(piece, start, count):
        return wbuf.at[piece, pl.ds(pl.multiple_of(start * block_rows, block_rows), count * block_rows)]

    def z_copy(piece, hops):
        ref = weight_ref_of(piece, arrival(me), 1)
        return send(ref, ref, z_send.at[piece, hops], z_recv.at[piece, z // planes], column, (me + 2 * hops) % seqs)

    def y_copy(piece, hops):
        ref = weight_ref_of(piece, core * chips + y * per, per)
        goal = (column + hops * ring) % columns
        return send(ref, ref, y_send.at[piece, hops], y_recv.at[piece, planes - hops], goal, me)

    def core_copy(piece):
        ref = weight_ref_of(piece, core * chips, chips)
        return send(ref, ref, b_send.at[piece], b_recv.at[piece], column, me + 1 - 2 * core)

    @pl.when(z % planes == y)
    def _():
        def plane_wait(k, _):
            src = (column + k) % columns
            send(wsend.at[0], wplane.at[src], p_send.at[0], p_recv.at[src], column, me).wait_recv()
            return 0

        lax.fori_loop(0, columns, plane_wait, 0)
        base_row = pl.multiple_of(arrival(me) * block_rows, block_rows)
        for group in range(3 * cols // 2):
            piece, lanes = weight_place(group)
            for i in range(wrows):
                wbuf[piece, pl.ds(base_row + i * columns, columns), lanes] = (
                    wplane[:, i, group, :].astype(jnp.bfloat16))
        for piece in range(PIECES):
            def z_start(hops, _):
                z_copy(piece, hops).start()
                return 0

            lax.fori_loop(1, chips, z_start, 0)

    def z_pass(piece):
        for m in range(per):
            source = m * planes + y

            @pl.when(source != z)
            def _():
                ref = weight_ref_of(piece, core * chips + y * per + m, 1)
                send(ref, ref, z_send.at[piece, 0], z_recv.at[piece, m], column, me).wait_recv()

        for hops in range(1, planes):
            y_copy(piece, hops).start()

    def y_pass(piece):
        for hops in range(1, planes):
            ref = weight_ref_of(piece, core * chips + (y + hops) % planes * per, per)
            send(ref, ref, y_send.at[piece, 0], y_recv.at[piece, hops], column, me).wait_recv()
        core_copy(piece).start()

    def core_wait(piece):
        ref = weight_ref_of(piece, (1 - core) * chips, chips)
        send(ref, ref, b_send.at[piece], b_recv.at[piece], column, me).wait_recv()

    def states_of(offset):
        return mod_all[pl.ds(slot(offset, 0), part_dev)].reshape(part_dev * rows, width)

    z_pass(0)
    z_pass(1)
    y_pass(0)
    z_pass(2)
    ring_copy(-1, 0, 0, right).wait_recv()
    ring_copy(-1, 0, 2, right).start()
    ring_copy(1, 1, 1, left).wait_recv()
    ring_copy(1, 1, 2, left).start()
    core_wait(0)
    project_kv(0, 0)
    y_pass(1)
    y_pass(2)
    core_wait(1)
    project_kv(0, 1)
    ring_copy(-1, 1, 0, right).wait_recv()
    ring_copy(1, 0, 1, left).wait_recv()
    for offset in (-1, 1):
        for group in range(cols // 2):
            project_kv(offset, group)
    for part in range(part_dev):
        ring_copy(2, part, 2, right).wait_recv()
    for group in range(cols // 2):
        project_kv(2, group)
    core_wait(PIECES - 1)
    for offset in (0, -1, 1, 2):
        project_q(offset)
        for part in range(part_dev):
            for head in range(cols):
                post(q_copy, q_own, slot(offset, part), head)

    text_copy.wait()
    kv_all[image:image + TEXT_PAD] = jnp.zeros((TEXT_PAD, 128), jnp.bfloat16)
    heads = lax.broadcasted_iota(jnp.int32, (txt, HEADS, 128), 1)
    mine = jnp.where(heads == x * cols + me // particles, text_buf[...].astype(jnp.float32), 0.0)
    kv_all[image:image + txt] = jnp.sum(mine, axis=1).astype(jnp.bfloat16)

    def kv_wait(k, _):
        src = (me + k) % seqs
        send(
            kv_out.at[0, 0], kv_all.at[pl.ds(pl.multiple_of(src * rows, rows), rows)],
            kv_send.at[0], kv_recv.at[src], column, me).wait_recv()
        return 0

    lax.fori_loop(0, seqs, kv_wait, 0)

    joint = image + TEXT_PAD
    bounds = [(low, min(KEYS, joint - low)) for low in range(0, joint, KEYS)]
    for low, count in bounds:
        turned = kv_all[low:low + count].astype(jnp.float32).T
        values_t[:, low:low + count] = turned[HD:2 * HD].astype(jnp.bfloat16)

    block = SLICES * rows
    factor = HD ** (-0.5) * LOG2E

    def o_copy(src, target):
        return send(o_out.at[src], o_all.at[me], o_send.at[src], o_recv.at[me], column, target)

    def fold(value, op):
        result = value[0:8]
        for row in range(8, value.shape[0], 8):
            result = op(result, value[row:row + 8])
        return result

    def attend(step, _):
        base = (me // SLICES + step) % (seqs // SLICES) * SLICES
        queries = []
        lower_lanes = low_lanes((half, 128))
        for side in range(SLICES):
            src = base + side
            send(q_out.at[0, 0], q_all.at[src], q_send.at[0], q_recv.at[src], column, me).wait_recv()
            packed = q_all[src].astype(jnp.float32)
            queries.append(jnp.where(lower_lanes, packed, 0.0).astype(jnp.bfloat16))
            queries.append(jnp.where(lower_lanes, swap_halves(packed), 0.0).astype(jnp.bfloat16))
        query = jnp.concatenate(queries, axis=0)
        top = jnp.full((8, block), -jnp.inf, jnp.float32)
        for low, count in bounds:
            part_scores = lax.dot_general(
                kv_all[low:low + count], query, (((1,), (1,)), ((), ())), preferred_element_type=jnp.float32)
            if low + count > image + txt:
                key = lax.broadcasted_iota(jnp.int32, part_scores.shape, 0) + low
                part_scores = jnp.where(key < image + txt, part_scores, -jnp.inf)
            scores[low:low + count] = part_scores
            top = jnp.maximum(top, fold(part_scores, jnp.maximum))
        top = jnp.max(top, axis=0, keepdims=True)
        total = jnp.zeros((8, block), jnp.float32)
        for low, count in bounds:
            expo = jnp.exp2((scores[low:low + count] - top) * factor)
            total = total + fold(expo, jnp.add)
            probs[low:low + count] = expo.astype(jnp.bfloat16)
        mixed = jnp.dot(values_t[...], probs[...], preferred_element_type=jnp.float32)
        result = (mixed / jnp.sum(total, axis=0, keepdims=True)).T
        for side in range(SLICES):
            target = base + side
            upper = result[side * rows:side * rows + half]
            lower = result[side * rows + half:(side + 1) * rows]
            o_out[target] = jnp.concatenate([upper, lower], axis=1).astype(jnp.bfloat16)

            @pl.when(target != me)
            def _():
                o_copy(target, target).start()

            @pl.when(target == me)
            def _():
                pltpu.make_async_copy(o_out.at[target], o_all.at[me], o_recv.at[me]).start()
        return 0

    lax.fori_loop(0, seqs // SLICES, attend, 0)

    def o_wait(k, _):
        src = (me + k) % seqs
        send(o_out.at[0], o_all.at[src], o_send.at[0], o_recv.at[src], column, me).wait_recv()
        return 0

    lax.fori_loop(0, seqs, o_wait, 0)
    low = low_lanes((half, 128))

    def final_copy(k):
        lanes = pl.ds(pl.multiple_of(x * (cols * HD), 128), cols * HD)
        return send(
            chosen.at[k], out_ref.at[:, :, lanes], f_send.at[k], f_recv.at[(ring - k) % ring],
            first + (x + k) % ring, me)

    for k in (2, 1, 3, 0):
        goal = (x + k) % ring
        for part in range(part_dev):
            source = anc_ref[(first + goal) * part_dev + part] % particles
            for group in range(cols // 2):
                even = o_all[2 * group * particles + source].astype(jnp.float32)
                odd = o_all[(2 * group + 1) * particles + source].astype(jnp.float32)
                lanes = slice(group * 128, (group + 1) * 128)
                chosen[k, part, 0:half, lanes] = jnp.where(low, even, swap_halves(odd)).astype(jnp.bfloat16)
                chosen[k, part, half:rows, lanes] = jnp.where(low, swap_halves(even), odd).astype(jnp.bfloat16)
        if k:
            final_copy(k).start()
    own_final = pltpu.make_async_copy(
        chosen.at[0], out_ref.at[:, :, pl.ds(pl.multiple_of(x * (cols * HD), 128), cols * HD)], f_send.at[0])
    own_final.start()
    own_final.wait()

    for part in range(part_dev):
        ring_copy(0, part, 0, right).wait_send()
        ring_copy(0, part, 1, left).wait_send()
    ring_copy(-1, 0, 2, right).wait_send()
    ring_copy(1, 1, 2, left).wait_send()

    for k in range(1, ring):
        plane_copy(k).wait_send()

    @pl.when(z % planes != y)
    def _():
        plane_copy(0).wait_send()

    for piece in range(PIECES):
        @pl.when(z % planes == y)
        def _():
            def z_sent(hops, _):
                z_copy(piece, hops).wait_send()
                return 0

            lax.fori_loop(1, chips, z_sent, 0)

        for hops in range(1, planes):
            y_copy(piece, hops).wait_send()
        core_copy(piece).wait_send()

    def item_sent(k, _):
        target = (me + k) % seqs
        part, head = target % particles, target // particles
        kv_copy(part, head).wait_send()
        q_copy(part, head).wait_send()
        o_copy(target, target).wait_send()
        return 0

    lax.fori_loop(1, seqs, item_sent, 0)
    for k in range(1, ring):
        final_copy(k).wait_send()
        lanes = pl.ds(pl.multiple_of((x + k) % ring * (cols * HD), 128), cols * HD)
        send(
            chosen.at[k], out_ref.at[:, :, lanes], f_send.at[k], f_recv.at[k],
            column, me).wait_recv()


def local(columns, seqs, latents, mod_table, step_index, qkv_weight, text_kv, ancestors):
    part_dev, rows, width = latents.shape
    ring = PER_PROMPT // part_dev
    cols = HEADS // ring
    txt = text_kv.shape[1]
    wrows = qkv_weight.shape[0]
    items = PER_PROMPT * cols
    joint = seqs * rows + TEXT_PAD
    bf16, f32 = jnp.bfloat16, jnp.float32
    vmem, dma = pltpu.VMEM, pltpu.SemaphoreType.DMA
    any_spec = pl.BlockSpec(memory_space=pl.ANY)
    smem_spec, vmem_spec = pl.BlockSpec(memory_space=pltpu.SMEM), pl.BlockSpec(memory_space=pltpu.VMEM)
    return pl.pallas_call(
        functools.partial(block_kernel, cols, ring, columns, seqs, txt),
        out_shape=jax.ShapeDtypeStruct((part_dev, rows, HEADS * HD), bf16),
        in_specs=[smem_spec, any_spec, any_spec, any_spec, vmem_spec, any_spec],
        out_specs=vmem_spec,
        scratch_shapes=[
            pltpu.SMEM(ancestors.shape, jnp.int32), vmem(latents.shape, bf16), vmem(mod_table.shape, f32), dma((3,)),
            vmem((PER_PROMPT, rows, width), bf16),
            vmem((width, width), bf16),
            vmem((ring, wrows, ROW_PAD, 128), f32),
            vmem((columns, wrows, ROW_PAD, 128), f32),
            vmem((PIECES, width, cols * HD), bf16),
            vmem((PER_PROMPT, cols, rows, 128), bf16),
            vmem((PER_PROMPT, cols, rows // 2, 128), bf16),
            vmem((joint, 128), bf16),
            vmem((HD, joint), bf16),
            vmem((seqs, rows // 2, 128), bf16),
            vmem((txt, HEADS, 128), bf16),
            vmem((joint, SLICES * rows), f32),
            vmem((joint, SLICES * rows), bf16),
            vmem((seqs, rows // 2, 128), bf16),
            vmem((seqs, rows // 2, 128), bf16),
            vmem((ring, part_dev, rows, cols * HD), bf16),
            dma((3, part_dev)), dma((3, part_dev)),
            dma((ring,)), dma((columns,)),
            dma((PIECES, seqs // 2)), dma((PIECES, seqs // 2 * ring // columns)),
            dma((PIECES, columns // ring)), dma((PIECES, columns // ring)), dma((PIECES,)), dma((PIECES,)), dma,
            dma((items,)), dma((items,)), dma((items,)), dma((items,)), dma((items,)), dma((items,)),
            dma((ring,)), dma((ring,)),
        ],
        compiler_params=pltpu.CompilerParams(
            collective_id=0, has_side_effects=True, vmem_limit_bytes=60 * 2**20),
        cost_estimate=pl.CostEstimate(flops=7 * 10**9, bytes_accessed=4 * 10**6, transcendentals=18 * 10**6),
        name="steered_block",
    )(step_index, ancestors, latents, mod_table, qkv_weight, text_kv.transpose(1, 0, 2))


def solution(mesh):
    in_specs = (P("particle", "seq", None), P(), P(), P(("particle", "seq"), None), P(), P())
    out_specs = P("particle", "seq", None)
    body = functools.partial(local, mesh.shape["particle"], mesh.shape["seq"])
    return jax.shard_map(body, mesh=mesh, in_specs=in_specs, out_specs=out_specs, check_vma=False)
```

```python
import functools

import jax
import jax.numpy as jnp
from jax import lax
from jax.experimental import pallas as pl
from jax.experimental.pallas import tpu as pltpu
from jax.sharding import PartitionSpec as P

HEADS = 16
HD = 64
PER_PROMPT = 8
MESH = pl.DeviceIdType.MESH
KEYS = 256
TEXT_PAD = 160
SLICES = 4
PIECES = 3
ROW_PAD = 8
LOG2E = 1.4426950408889634


def low_lanes(shape):
    return lax.broadcasted_iota(jnp.int32, shape, len(shape) - 1) < HD


def swap_halves(value):
    return pltpu.roll(value, HD, len(value.shape) - 1)


def send(src, dst, send_sem, recv_sem, column, seq):
    return pltpu.make_async_remote_copy(
        src_ref=src, dst_ref=dst, send_sem=send_sem, recv_sem=recv_sem,
        device_id=(column, seq), device_id_type=MESH,
    )


def pack_weight(weight_ref, wsend, ring, cols):
    shard = weight_ref[...].astype(jnp.float32)
    count = shard.shape[0]
    for r in range(ring):
        for group in range(3 * cols // 2):
            if group < cols // 2:
                start = (r * cols + 2 * group) * 3 * HD
                piece = jnp.concatenate([shard[:, start:start + HD], shard[:, start + 3 * HD:start + 4 * HD]], axis=1)
            else:
                start = (r * cols + group - cols // 2) * 3 * HD + HD
                piece = shard[:, start:start + 2 * HD]
            for i in range(count):
                wsend[r, i, group:group + 1, :] = piece[i:i + 1]


def block_kernel(
    cols, ring, columns, seqs, txt,
    step_ref, anc_any, lat_any, mod_any, weight_ref, text_hbm, out_ref,
    anc_ref, lat_ref, mod_ref, in_sem, mod_all, order, wsend, wplane, wbuf, kv_out, q_out, kv_all, values_t, q_all, text_buf,
    scores, probs, o_out, o_all, chosen,
    x_send, x_recv, p_send, p_recv, z_send, z_recv, y_send, y_recv, b_send, b_recv, t_sem,
    kv_send, kv_recv, q_send, q_recv, o_send, o_recv, f_send, f_recv,
):
    part_dev, rows, width = lat_ref.shape
    particles = ring * part_dev
    half = rows // 2
    column, me = lax.axis_index("particle"), lax.axis_index("seq")
    first, x = column // ring * ring, column % ring
    left, right = first + (x + ring - 1) % ring, first + (x + 1) % ring
    wrows = weight_ref.shape[0]
    image = seqs * rows

    inputs = [
        pltpu.make_async_copy(src, dst, in_sem.at[i])
        for i, (src, dst) in enumerate(((lat_any, lat_ref), (mod_any, mod_ref), (anc_any, anc_ref)))
    ]
    for copy in inputs:
        copy.start()

    barrier = pltpu.get_barrier_semaphore()

    def greet_seq(k, _):
        pl.semaphore_signal(barrier, inc=1, device_id=(column, (me + k) % seqs), device_id_type=MESH)
        return 0

    def greet_column(k, _):
        pl.semaphore_signal(barrier, inc=1, device_id=((column + k) % columns, me), device_id_type=MESH)
        return 0

    lax.fori_loop(1, seqs, greet_seq, 0)
    lax.fori_loop(1, columns, greet_column, 0)

    text_block = pl.ds(pl.multiple_of(column // ring * HEADS, HEADS), HEADS)
    text_copy = pltpu.make_async_copy(text_hbm.at[:, text_block, :], text_buf, t_sem)
    text_copy.start()
    pack_weight(weight_ref, wsend, ring, cols)
    span = seqs * wrows
    chips, planes = seqs // 2, columns // ring
    per = chips // planes
    y, z, core = column // ring, me // 2, me % 2

    def arrival(index):
        at = index // 2
        return index % 2 * chips + at % planes * per + at // planes

    local_row = lax.broadcasted_iota(jnp.int32, (span, 1), 0)
    owner = lax.shift_right_logical(local_row * 43691, 17)
    place = arrival(owner) * (wrows * columns) + (local_row - owner * wrows) * columns
    lane = lax.broadcasted_iota(jnp.int32, (span, width), 1)
    for c in range(columns):
        order[c * span:(c + 1) * span] = jnp.where(lane == place + c, 1.0, 0.0).astype(jnp.bfloat16)
    pl.semaphore_wait(barrier, seqs + columns - 2)

    def plane_copy(k):
        goal = (x + k) % ring
        return send(
            wsend.at[goal], wplane.at[column], p_send.at[k], p_recv.at[column], z % planes * ring + goal, me)

    for k in range(1, ring):
        plane_copy(k).start()

    @pl.when(z % planes != y)
    def _():
        plane_copy(0).start()

    @pl.when(z % planes == y)
    def _():
        pltpu.make_async_copy(wsend.at[x], wplane.at[column], p_recv.at[column]).start()

    def slot(offset, part):
        return ((x + offset + ring) % ring) * part_dev + part

    def ring_copy(offset, part, leg, target):
        ref = mod_all.at[slot(offset, part)]
        return send(ref, ref, x_send.at[leg, part], x_recv.at[leg, part], target, me)

    for copy in inputs:
        copy.wait()
    mod_row = mod_ref[pl.ds(step_ref[0], 1), :]
    shift, scale = mod_row[:, 0:width], mod_row[:, width:2 * width]
    for part in range(part_dev):
        values = lat_ref[part].astype(jnp.float32)
        mean = jnp.mean(values, axis=-1, keepdims=True)
        centred = values - mean
        var = jnp.mean(centred * centred, axis=-1, keepdims=True)
        normed = centred / jnp.sqrt(var + 1e-06)
        modded = (normed * (1.0 + scale) + shift).astype(jnp.bfloat16)
        mod_all[slot(0, part)] = jnp.dot(modded, order[...], preferred_element_type=jnp.float32).astype(jnp.bfloat16)
    for part in range(part_dev):
        ring_copy(0, part, 0, right).start()
        ring_copy(0, part_dev - 1 - part, 1, left).start()

    def item_seq(part, head):
        position, which = part // 2, part % 2
        chip = which * (chips // 2) + head % 2 * (chips // 4) + head // 2 * 2 + position // 2
        return chip * 2 + position % 2

    def item_of(target):
        chip = target // 2
        head = chip // (chips // 4) % 2 + chip // 2 % 2 * 2
        return (chip % 2 * 2 + target % 2) * 2 + chip // (chips // 2), head

    def kv_copy(part, head):
        return send(
            kv_out.at[part, head], kv_all.at[pl.ds(pl.multiple_of(me * rows, rows), rows)],
            kv_send.at[item_seq(part, head)], kv_recv.at[me], column, item_seq(part, head),
        )

    def q_copy(part, head):
        return send(
            q_out.at[part, head], q_all.at[me],
            q_send.at[item_seq(part, head)], q_recv.at[me], column, item_seq(part, head),
        )

    def post(copy, own, part, head):
        target = item_seq(part, head)

        @pl.when(target != me)
        def _():
            copy(part, head).start()

        @pl.when(target == me)
        def _():
            own(part, head).start()

    def kv_own(part, head):
        return pltpu.make_async_copy(
            kv_out.at[part, head], kv_all.at[pl.ds(pl.multiple_of(me * rows, rows), rows)], kv_recv.at[me])

    def q_own(part, head):
        return pltpu.make_async_copy(q_out.at[part, head], q_all.at[me], q_recv.at[me])

    def project_kv(offset, group):
        base = slot(offset, 0)
        kv = jnp.dot(states_of(offset), wbuf[group], preferred_element_type=jnp.float32)
        for part in range(part_dev):
            for side in range(2):
                piece = kv[part * rows:(part + 1) * rows, side * 128:(side + 1) * 128]
                kv_out[base + part, 2 * group + side] = piece.astype(jnp.bfloat16)
                post(kv_copy, kv_own, base + part, 2 * group + side)

    def project_q(offset):
        base = slot(offset, 0)
        query = jnp.dot(states_of(offset), wbuf[PIECES - 1], preferred_element_type=jnp.float32)
        low = low_lanes((half, 128))
        for part in range(part_dev):
            for group in range(cols // 2):
                lanes = slice(group * 128, (group + 1) * 128)
                upper = query[part * rows:part * rows + half, lanes]
                lower = query[part * rows + half:(part + 1) * rows, lanes]
                q_out[base + part, 2 * group] = jnp.where(low, upper, swap_halves(lower)).astype(jnp.bfloat16)
                q_out[base + part, 2 * group + 1] = jnp.where(low, swap_halves(upper), lower).astype(jnp.bfloat16)

    def weight_place(group):
        if group < cols // 2:
            return PIECES - 1, slice(group * 128, (group + 1) * 128)
        head = group - cols // 2
        return head // 2, slice(head % 2 * 128, (head % 2 + 1) * 128)

    block_rows = wrows * columns

    def weight_ref_of(piece, start, count):
        return wbuf.at[piece, pl.ds(pl.multiple_of(start * block_rows, block_rows), count * block_rows)]

    def z_copy(piece, hops):
        ref = weight_ref_of(piece, arrival(me), 1)
        return send(ref, ref, z_send.at[piece, hops], z_recv.at[piece, z // planes], column, (me + 2 * hops) % seqs)

    def y_copy(piece, hops):
        ref = weight_ref_of(piece, core * chips + y * per, per)
        goal = (column + hops * ring) % columns
        return send(ref, ref, y_send.at[piece, hops], y_recv.at[piece, planes - hops], goal, me)

    def core_copy(piece):
        ref = weight_ref_of(piece, core * chips, chips)
        return send(ref, ref, b_send.at[piece], b_recv.at[piece], column, me + 1 - 2 * core)

    @pl.when(z % planes == y)
    def _():
        def plane_wait(k, _):
            src = (column + k) % columns
            send(wsend.at[0], wplane.at[src], p_send.at[0], p_recv.at[src], column, me).wait_recv()
            return 0

        lax.fori_loop(0, columns, plane_wait, 0)
        base_row = pl.multiple_of(arrival(me) * block_rows, block_rows)
        for group in range(3 * cols // 2):
            piece, lanes = weight_place(group)
            for i in range(wrows):
                wbuf[piece, pl.ds(base_row + i * columns, columns), lanes] = (
                    wplane[:, i, group, :].astype(jnp.bfloat16))
        for piece in range(PIECES):
            def z_start(hops, _):
                z_copy(piece, hops).start()
                return 0

            lax.fori_loop(1, chips, z_start, 0)

    def z_pass(piece):
        for m in range(per):
            source = m * planes + y

            @pl.when(source != z)
            def _():
                ref = weight_ref_of(piece, core * chips + y * per + m, 1)
                send(ref, ref, z_send.at[piece, 0], z_recv.at[piece, m], column, me).wait_recv()

        for hops in range(1, planes):
            y_copy(piece, hops).start()

    def y_pass(piece):
        for hops in range(1, planes):
            ref = weight_ref_of(piece, core * chips + (y + hops) % planes * per, per)
            send(ref, ref, y_send.at[piece, 0], y_recv.at[piece, hops], column, me).wait_recv()
        core_copy(piece).start()

    def core_wait(piece):
        ref = weight_ref_of(piece, (1 - core) * chips, chips)
        send(ref, ref, b_send.at[piece], b_recv.at[piece], column, me).wait_recv()

    def states_of(offset):
        return mod_all[pl.ds(slot(offset, 0), part_dev)].reshape(part_dev * rows, width)

    z_pass(0)
    z_pass(1)
    y_pass(0)
    z_pass(2)
    ring_copy(-1, 0, 0, right).wait_recv()
    ring_copy(-1, 0, 2, right).start()
    ring_copy(1, 1, 1, left).wait_recv()
    ring_copy(1, 1, 2, left).start()
    core_wait(0)
    project_kv(0, 0)
    y_pass(1)
    y_pass(2)
    core_wait(1)
    project_kv(0, 1)
    ring_copy(-1, 1, 0, right).wait_recv()
    ring_copy(1, 0, 1, left).wait_recv()
    for offset in (-1, 1):
        for group in range(cols // 2):
            project_kv(offset, group)
    for part in range(part_dev):
        ring_copy(2, part, 2, right).wait_recv()
    for group in range(cols // 2):
        project_kv(2, group)
    core_wait(PIECES - 1)
    for offset in (0, -1, 1, 2):
        project_q(offset)
        for part in range(part_dev):
            for head in range(cols):
                post(q_copy, q_own, slot(offset, part), head)

    text_copy.wait()
    kv_all[image:image + TEXT_PAD] = jnp.zeros((TEXT_PAD, 128), jnp.bfloat16)
    heads = lax.broadcasted_iota(jnp.int32, (txt, HEADS, 128), 1)
    mine = jnp.where(heads == x * cols + item_of(me)[1], text_buf[...].astype(jnp.float32), 0.0)
    kv_all[image:image + txt] = jnp.sum(mine, axis=1).astype(jnp.bfloat16)

    def kv_wait(k, _):
        src = (me + k) % seqs
        send(
            kv_out.at[0, 0], kv_all.at[pl.ds(pl.multiple_of(src * rows, rows), rows)],
            kv_send.at[0], kv_recv.at[src], column, me).wait_recv()
        return 0

    lax.fori_loop(0, seqs, kv_wait, 0)

    joint = image + TEXT_PAD
    bounds = [(low, min(KEYS, joint - low)) for low in range(0, joint, KEYS)]
    for low, count in bounds:
        turned = kv_all[low:low + count].astype(jnp.float32).T
        values_t[:, low:low + count] = turned[HD:2 * HD].astype(jnp.bfloat16)

    block = SLICES * rows
    factor = HD ** (-0.5) * LOG2E

    def o_copy(src, target):
        return send(o_out.at[src], o_all.at[me], o_send.at[src], o_recv.at[me], column, target)

    def fold(value, op):
        result = value[0:8]
        for row in range(8, value.shape[0], 8):
            result = op(result, value[row:row + 8])
        return result

    def attend(step, _):
        groups = seqs // SLICES
        base = (me // SLICES + groups + step * (1 - 2 * core)) % groups * SLICES
        queries = []
        lower_lanes = low_lanes((half, 128))
        for side in range(SLICES):
            src = base + side
            send(q_out.at[0, 0], q_all.at[src], q_send.at[0], q_recv.at[src], column, me).wait_recv()
            packed = q_all[src].astype(jnp.float32)
            queries.append(jnp.where(lower_lanes, packed, 0.0).astype(jnp.bfloat16))
            queries.append(jnp.where(lower_lanes, swap_halves(packed), 0.0).astype(jnp.bfloat16))
        query = jnp.concatenate(queries, axis=0)
        top = jnp.full((8, block), -jnp.inf, jnp.float32)
        for low, count in bounds:
            part_scores = lax.dot_general(
                kv_all[low:low + count], query, (((1,), (1,)), ((), ())), preferred_element_type=jnp.float32)
            if low + count > image + txt:
                key = lax.broadcasted_iota(jnp.int32, part_scores.shape, 0) + low
                part_scores = jnp.where(key < image + txt, part_scores, -jnp.inf)
            scores[low:low + count] = part_scores
            top = jnp.maximum(top, fold(part_scores, jnp.maximum))
        top = jnp.max(top, axis=0, keepdims=True)
        total = jnp.zeros((8, block), jnp.float32)
        for low, count in bounds:
            expo = jnp.exp2((scores[low:low + count] - top) * factor)
            total = total + fold(expo, jnp.add)
            probs[low:low + count] = expo.astype(jnp.bfloat16)
        mixed = jnp.dot(values_t[...], probs[...], preferred_element_type=jnp.float32)
        result = (mixed / jnp.sum(total, axis=0, keepdims=True)).T
        for side in range(SLICES):
            target = base + side
            upper = result[side * rows:side * rows + half]
            lower = result[side * rows + half:(side + 1) * rows]
            o_out[target] = jnp.concatenate([upper, lower], axis=1).astype(jnp.bfloat16)

            @pl.when(target != me)
            def _():
                o_copy(target, target).start()

            @pl.when(target == me)
            def _():
                pltpu.make_async_copy(o_out.at[target], o_all.at[me], o_recv.at[me]).start()
        return 0

    lax.fori_loop(0, seqs // SLICES, attend, 0)

    def o_wait(k, _):
        src = (me + k) % seqs
        send(o_out.at[0], o_all.at[src], o_send.at[0], o_recv.at[src], column, me).wait_recv()
        return 0

    lax.fori_loop(0, seqs, o_wait, 0)
    low = low_lanes((half, 128))

    def final_copy(k):
        lanes = pl.ds(pl.multiple_of(x * (cols * HD), 128), cols * HD)
        return send(
            chosen.at[k], out_ref.at[:, :, lanes], f_send.at[k], f_recv.at[(ring - k) % ring],
            first + (x + k) % ring, me)

    for k in (2, 1, 3, 0):
        goal = (x + k) % ring
        for part in range(part_dev):
            source = anc_ref[(first + goal) * part_dev + part] % particles
            for group in range(cols // 2):
                even = o_all[item_seq(source, 2 * group)].astype(jnp.float32)
                odd = o_all[item_seq(source, 2 * group + 1)].astype(jnp.float32)
                lanes = slice(group * 128, (group + 1) * 128)
                chosen[k, part, 0:half, lanes] = jnp.where(low, even, swap_halves(odd)).astype(jnp.bfloat16)
                chosen[k, part, half:rows, lanes] = jnp.where(low, swap_halves(even), odd).astype(jnp.bfloat16)
        if k:
            final_copy(k).start()
    own_final = pltpu.make_async_copy(
        chosen.at[0], out_ref.at[:, :, pl.ds(pl.multiple_of(x * (cols * HD), 128), cols * HD)], f_send.at[0])
    own_final.start()
    own_final.wait()

    for part in range(part_dev):
        ring_copy(0, part, 0, right).wait_send()
        ring_copy(0, part, 1, left).wait_send()
    ring_copy(-1, 0, 2, right).wait_send()
    ring_copy(1, 1, 2, left).wait_send()

    for k in range(1, ring):
        plane_copy(k).wait_send()

    @pl.when(z % planes != y)
    def _():
        plane_copy(0).wait_send()

    for piece in range(PIECES):
        @pl.when(z % planes == y)
        def _():
            def z_sent(hops, _):
                z_copy(piece, hops).wait_send()
                return 0

            lax.fori_loop(1, chips, z_sent, 0)

        for hops in range(1, planes):
            y_copy(piece, hops).wait_send()
        core_copy(piece).wait_send()

    def item_sent(k, _):
        target = (me + k) % seqs
        part, head = item_of(target)
        kv_copy(part, head).wait_send()
        q_copy(part, head).wait_send()
        o_copy(target, target).wait_send()
        return 0

    lax.fori_loop(1, seqs, item_sent, 0)
    for k in range(1, ring):
        final_copy(k).wait_send()
        lanes = pl.ds(pl.multiple_of((x + k) % ring * (cols * HD), 128), cols * HD)
        send(
            chosen.at[k], out_ref.at[:, :, lanes], f_send.at[k], f_recv.at[k],
            column, me).wait_recv()


def local(columns, seqs, latents, mod_table, step_index, qkv_weight, text_kv, ancestors):
    part_dev, rows, width = latents.shape
    ring = PER_PROMPT // part_dev
    cols = HEADS // ring
    txt = text_kv.shape[1]
    wrows = qkv_weight.shape[0]
    items = PER_PROMPT * cols
    joint = seqs * rows + TEXT_PAD
    bf16, f32 = jnp.bfloat16, jnp.float32
    vmem, dma = pltpu.VMEM, pltpu.SemaphoreType.DMA
    any_spec = pl.BlockSpec(memory_space=pl.ANY)
    smem_spec, vmem_spec = pl.BlockSpec(memory_space=pltpu.SMEM), pl.BlockSpec(memory_space=pltpu.VMEM)
    return pl.pallas_call(
        functools.partial(block_kernel, cols, ring, columns, seqs, txt),
        out_shape=jax.ShapeDtypeStruct((part_dev, rows, HEADS * HD), bf16),
        in_specs=[smem_spec, any_spec, any_spec, any_spec, vmem_spec, any_spec],
        out_specs=vmem_spec,
        scratch_shapes=[
            pltpu.SMEM(ancestors.shape, jnp.int32), vmem(latents.shape, bf16), vmem(mod_table.shape, f32), dma((3,)),
            vmem((PER_PROMPT, rows, width), bf16),
            vmem((width, width), bf16),
            vmem((ring, wrows, ROW_PAD, 128), f32),
            vmem((columns, wrows, ROW_PAD, 128), f32),
            vmem((PIECES, width, cols * HD), bf16),
            vmem((PER_PROMPT, cols, rows, 128), bf16),
            vmem((PER_PROMPT, cols, rows // 2, 128), bf16),
            vmem((joint, 128), bf16),
            vmem((HD, joint), bf16),
            vmem((seqs, rows // 2, 128), bf16),
            vmem((txt, HEADS, 128), bf16),
            vmem((joint, SLICES * rows), f32),
            vmem((joint, SLICES * rows), bf16),
            vmem((seqs, rows // 2, 128), bf16),
            vmem((seqs, rows // 2, 128), bf16),
            vmem((ring, part_dev, rows, cols * HD), bf16),
            dma((3, part_dev)), dma((3, part_dev)),
            dma((ring,)), dma((columns,)),
            dma((PIECES, seqs // 2)), dma((PIECES, seqs // 2 * ring // columns)),
            dma((PIECES, columns // ring)), dma((PIECES, columns // ring)), dma((PIECES,)), dma((PIECES,)), dma,
            dma((items,)), dma((items,)), dma((items,)), dma((items,)), dma((items,)), dma((items,)),
            dma((ring,)), dma((ring,)),
        ],
        compiler_params=pltpu.CompilerParams(
            collective_id=0, has_side_effects=True, vmem_limit_bytes=60 * 2**20),
        cost_estimate=pl.CostEstimate(flops=7 * 10**9, bytes_accessed=4 * 10**6, transcendentals=18 * 10**6),
        name="steered_block",
    )(step_index, ancestors, latents, mod_table, qkv_weight, text_kv.transpose(1, 0, 2))


def solution(mesh):
    in_specs = (P("particle", "seq", None), P(), P(), P(("particle", "seq"), None), P(), P())
    out_specs = P("particle", "seq", None)
    body = functools.partial(local, mesh.shape["particle"], mesh.shape["seq"])
    return jax.shard_map(body, mesh=mesh, in_specs=in_specs, out_specs=out_specs, check_vma=False)
```
